32 devices in a mesh: groups: 2 (over y), blk: 4 (over z), heads: 2 (over x), beam: 2 (over core).
Axes of the slice: x: 2, y: 2, z: 4, core: 2. Of those that a mesh axis runs over, the one named last changes fastest.
Arguments:
- queries: bfloat16 [4, 32, 64, 128], P(('groups', 'beam'), 'blk', 'heads'), parts along dimension 0, may hold values from -110 to 110
- positions: int32 [4, 32], P(('groups', 'beam'), 'blk'), parts along dimension 0, may hold values from 512 to 4096
- row_order: int32 [4, 32], P(('groups', 'beam')), parts along dimension 0, may hold values from 0 to 31, each once within a row
- lengths: int32 [8], P(('groups', 'blk')), parts along dimension 0, may hold values from 128 to 1024
- cache_keys: bfloat16 [8, 4, 1024, 128], P(('groups', 'blk'), 'heads'), parts along dimension 0, may hold values from -4 to 4
- cache_values: bfloat16 [8, 4, 1024, 128], P(('groups', 'blk'), 'heads'), parts along dimension 0, may hold values from -6 to 6
Outputs:
- attended: bfloat16 [4, 32, 64, 128], P(('groups', 'beam'), 'blk', 'heads'), parts along dimension 0
The draws below stay inside these ranges and needn't reach their ends.
There are 2 independent parts, one for each index of `groups`. The reference program is written for one: setup_inputs(seed, part) draws one part's arguments, and reference() takes and returns one part's arrays. A program takes and returns all parts, laid end to end along the dimension named above; each array names one. Nothing has to cross between parts.
Inputs may be any that keep to these rules, and one draw needn't show every extreme that they name: Slots of shard s from lengths[s] on hold no cache entry. `positions`: a row reads the cache entries whose global position, counted shard after shard as in the reference program, lies below its position. row_order[e] is a permutation of 0 to 31.
All inputs are finite; a program needn't handle non-finite values.
Results may differ from the reference program's by a relative error of at most 0.0015.
Values may be sent and summed in bfloat16 or wider, within the bound.
No kernel may reach another device: no remote copies, remote signals or barrier semaphores. Data moves between devices by JAX's collectives and lax.ppermute only.
A program may use at most 64 MiB of HBM per device.

```python
import math
import jax
import jax.numpy as jnp
from jax import lax

HQ = 64
KVH = 4
HD = 128
CAP = 1024
KB = 256
GQ = 16
SETS = 2
SHARDS = 4
ROWS_SET = 32
CONTEXT = 4096


def base_keys(key):
    drawn = jax.random.normal(jax.random.fold_in(key, 11), (SHARDS, KVH, CAP, HD), jnp.float32)
    drawn = jnp.clip(drawn, -4.0, 4.0)
    return drawn


def draw_cache_keys(key, part):
    return base_keys(key).astype(jnp.bfloat16)


def draw_queries(key, part):
    full_shape = (SETS, ROWS_SET, HQ, HD)
    scales = jnp.exp(jax.random.uniform(jax.random.fold_in(key, 26), (SETS, ROWS_SET, HQ, 1), jnp.float32, 0.0, math.log(12.0)))
    entries = jnp.clip(2.5 * scales * jax.random.normal(jax.random.fold_in(key, 25), full_shape, jnp.float32), -110.0, 110.0)
    return entries.astype(jnp.bfloat16)


def plant(values, key, low, largest):
    extent = values.shape
    index_at = [jax.random.randint(jax.random.fold_in(key, axis), (), 0, extent[axis]) for axis in range(len(extent))]
    values = values.at[tuple(index_at)].set(low)
    longest = extent.index(max(extent))
    index_at[longest] = (index_at[longest] + 1) % extent[longest]
    return values.at[tuple(index_at)].set(largest)


def levels(rng, shape, pieces, low, high):
    factor_of = 1.0
    for axis_at, blocks in pieces:
        draws = jax.random.uniform(jax.random.fold_in(jax.random.fold_in(rng, 6), axis_at), (blocks,), jnp.float32, low / len(pieces), high / len(pieces))
        factor_of = factor_of * jnp.repeat(jnp.exp(draws), shape[axis_at] // blocks).reshape((-1,) + (1,) * (len(shape) - 1 - axis_at))
    return factor_of


def bell_draw(rng, dims, width, reach, pieces=(), kind=jnp.bfloat16):
    level = levels(rng, dims, pieces, -0.22, 0.18) if pieces else 1.0
    values = jax.random.normal(rng, dims, jnp.float32) * width * level
    return jnp.minimum(jnp.maximum(values, -reach), reach).astype(kind)


def setup_inputs(seed: int = 0, part: int = 0) -> dict:
    key_list = jax.random.split(jax.random.key(seed), 7)
    own_keys = jax.random.split(jax.random.fold_in(key_list[6], part), 7)
    return {
        "queries": draw_queries(jax.random.fold_in(jax.random.fold_in(key_list[6], part), 71), part),
        "positions": plant(jax.random.randint(own_keys[1], (SETS, ROWS_SET), CONTEXT // 8, CONTEXT + 1), jax.random.fold_in(own_keys[1], 1), CONTEXT // 8, CONTEXT).astype(jnp.int32),
        "row_order": jax.vmap(lambda own: jax.random.permutation(own, ROWS_SET))(jax.random.split(own_keys[2], SETS)).reshape((SETS, ROWS_SET)).astype(jnp.int32),
        "lengths": plant(jax.random.randint(own_keys[3], (SHARDS,), CAP // 8, CAP + 1), jax.random.fold_in(own_keys[3], 1), CAP // 8, CAP).astype(jnp.int32),
        "cache_keys": draw_cache_keys(jax.random.fold_in(jax.random.fold_in(key_list[6], part), 71), part),
        "cache_values": bell_draw(own_keys[5], (SHARDS, KVH, CAP, HD), 1.0, 6.0, ((0, 4), (1, 2))),
    }


masked_score = -1.0e30


def combine_parts(running, latest):
    run_out, run_tot, run_top = running
    new_out, new_tot, new_top = latest
    joined = jnp.maximum(run_top, new_top)
    older = jnp.exp(run_top - joined)
    newer = jnp.exp(new_top - joined)
    return (run_out * older[..., None] + new_out * newer[..., None], run_tot * older + new_tot * newer, joined)


def reference(queries, positions, row_order, lengths, cache_keys, cache_values):
    scaling = float(HD) ** -0.5
    offsets = (jnp.cumsum(lengths) - lengths).astype(jnp.int32)
    query_all = queries.astype(jnp.float32).reshape(SETS, ROWS_SET, KVH, GQ, HD)
    initial = (jnp.zeros((SETS, ROWS_SET, KVH, GQ, HD), jnp.float32),
               jnp.zeros((SETS, ROWS_SET, KVH, GQ), jnp.float32),
               jnp.full((SETS, ROWS_SET, KVH, GQ), masked_score, jnp.float32))

    def per_shard(running, shard_data):
        key_shard, value_shard, offset, length = shard_data
        for block in range(CAP // KB):
            first_slot = block * KB
            key_block = key_shard[:, first_slot:first_slot + KB].astype(jnp.float32)
            value_block = value_shard[:, first_slot:first_slot + KB].astype(jnp.float32)
            scores = jnp.einsum("erkgd,kjd->erkgj", query_all, key_block) * scaling
            slot_ids = first_slot + jnp.arange(KB, dtype=jnp.int32)
            visible = (slot_ids < length)[None, None, :] & ((offset + slot_ids)[None, None, :] < positions[:, :, None])
            visible = visible[:, :, None, None, :]
            highest = jnp.max(jnp.where(visible, scores, masked_score), axis=-1)
            weights = jnp.where(visible, jnp.exp(scores - highest[..., None]), 0.0)
            totals = jnp.sum(weights, axis=-1)
            rounded = lax.optimization_barrier(weights.astype(jnp.bfloat16)).astype(jnp.float32)
            block_out = jnp.einsum("erkgj,kjd->erkgd", rounded, value_block)
            running = combine_parts(running, (block_out, totals, highest))
        return running, None

    final, unused = lax.scan(per_shard, initial, (cache_keys, cache_values, offsets, lengths))
    result = final[0] / final[1][..., None]
    result = result.reshape(SETS, ROWS_SET, HQ, HD)
    placed = jax.vmap(lambda chosen, indices: chosen[indices])(result, row_order.astype(jnp.int32))
    return placed.astype(jnp.bfloat16)
```

```python
import functools

import jax
import jax.numpy as jnp
from jax import lax
from jax.experimental import pallas as pl
from jax.experimental.pallas import tpu as pltpu
from jax.sharding import PartitionSpec as P

KB = 256
LANES = 128
MASKED = -1e30
LOW = -32768.0
FINE = 32768.0
STEPS = 32767.0
SCALE_GRID = 1024.0
STATS = 16

VMEM = pl.BlockSpec(memory_space=pltpu.VMEM)
SMEM = pl.BlockSpec(memory_space=pltpu.SMEM)


def partner_pairs(count, step):
    if count & (count - 1) == 0:
        return [(i, i ^ step) for i in range(count)]
    return [(i, (i + step) % count) for i in range(count)]


def send_to(me, count, step):
    return (me ^ step) if count & (count - 1) == 0 else lax.rem(me + step, count)


def got_from(me, count, step):
    return (me ^ step) if count & (count - 1) == 0 else lax.rem(me - step + count, count)


def pack_kernel(positions_ref, lengths_ref, queries_ref, packed_ref, *, tiles):
    rows, heads, width = queries_ref.shape[1:]
    me = lax.axis_index("blk")
    packed_ref[: rows * heads] = queries_ref[0].reshape(rows * heads, width)
    digit = lax.broadcasted_iota(jnp.int32, (16, LANES), 0)
    lane = lax.broadcasted_iota(jnp.int32, (16, LANES), 1)
    own_length = lengths_ref[0]
    for tile in range(tiles):
        place = lane + tile * LANES
        held = jnp.zeros((16, LANES), jnp.int32)
        for row in range(rows):
            held = jnp.where(place == me * rows + row, positions_ref[0, row], held)
        sized = jnp.where(place == me, own_length, 0)
        digits = jnp.where(digit < 3, held, sized)
        third = jnp.where(digit < 3, digit, digit - 3)
        digits = jnp.where(
            third == 0, digits >> 14, jnp.where(third == 1, (digits >> 7) & 127, digits & 127)
        )
        digits = jnp.where(digit < 6, digits, 0)
        packed_ref[pl.ds(rows * heads + tile * 16, 16)] = digits.astype(jnp.float32).astype(jnp.bfloat16)


def attend_kernel(*refs, count, steps, rows, kv_heads, group, tiles, scaling):
    order_ref, lengths_ref, keys_ref, values_ref = refs[:4]
    message_refs = refs[4 : 4 + count]
    out_refs = refs[4 + count : 4 + count + len(steps)]
    held, picked = refs[4 + count + len(steps) :]
    me = lax.axis_index("blk")
    heads = kv_heads * group
    body = rows * heads
    capacity = keys_ref.shape[2]
    for step in range(count):
        held[got_from(me, count, step)] = message_refs[step][...]
    pos, offset = [], jnp.zeros((1, 1), jnp.float32)
    for tile in range(tiles):
        digits = held[0, pl.ds(body + tile * 16, 16)].astype(jnp.float32)
        for other in range(1, count):
            digits += held[other, pl.ds(body + tile * 16, 16)].astype(jnp.float32)
        pos.append(digits[0:1] * 16384.0 + digits[1:2] * 128.0 + digits[2:3])
        sizes = digits[3:4] * 16384.0 + digits[4:5] * 128.0 + digits[5:6]
        lane = lax.broadcasted_iota(jnp.int32, (1, LANES), 1) + tile * LANES
        offset += jnp.sum(jnp.where(lane < me, sizes, 0.0), axis=1, keepdims=True)
    own_length = lengths_ref[0].astype(jnp.float32)
    live = [jnp.clip(p - offset, 0.0, own_length) for p in pos]
    high = [jnp.floor(x * (1.0 / 128.0)) for x in live]
    low = [x - h * 128.0 for x, h in zip(live, high)]
    live_digits = jnp.concatenate(
        [jnp.concatenate([h, l, jnp.zeros((6, LANES), jnp.float32)], axis=0) for h, l in zip(high, low)],
        axis=1,
    ).astype(jnp.bfloat16)
    columns = rows * group
    lane_row = lax.broadcasted_iota(jnp.int32, (1, columns), 1) // group
    spread_row = lax.broadcasted_iota(jnp.int32, (tiles * LANES, columns), 0)
    counts = []
    for at, step in enumerate(steps):
        target = send_to(me, count, step)
        chosen = jnp.zeros((1, columns), jnp.int32)
        for i in range(rows):
            row = order_ref[0, target * rows + i]
            chosen = jnp.where(lane_row == i, row, chosen)
            source = row // rows
            inner = row - source * rows
            for kv in range(kv_heads):
                start = pl.multiple_of(inner * heads + kv * group, group)
                picked[kv, pl.ds(at * columns + i * group, group)] = held[source, pl.ds(start, group)]
        spread = jnp.where(spread_row == chosen, 1.0, 0.0).astype(jnp.bfloat16)
        both = jnp.dot(live_digits, spread, preferred_element_type=jnp.float32)
        counts.append((both[0:1] * 128.0 + both[1:2]).astype(jnp.int32))
    visible_count = jnp.concatenate(counts, axis=1) if len(counts) > 1 else counts[0]

    wide = len(steps) * columns
    slot = lax.broadcasted_iota(jnp.int32, (KB, wide), 0)
    for kv in range(kv_heads):
        query = picked[kv]
        top = jnp.full((1, wide), MASKED, jnp.float32)
        total = jnp.zeros((1, wide), jnp.float32)
        out = jnp.zeros((values_ref.shape[3], wide), jnp.float32)
        for block in range(capacity // KB):
            key_block = keys_ref[0, kv, block * KB : (block + 1) * KB]
            value_block = values_ref[0, kv, block * KB : (block + 1) * KB]
            scores = lax.dot_general(
                key_block, query, (((1,), (1,)), ((), ())), preferred_element_type=jnp.float32
            )
            scores = jnp.where(slot < visible_count - block * KB, scores, MASKED)
            block_top = jnp.max(scores, axis=0, keepdims=True)
            weights = jnp.exp((scores - block_top) * scaling)
            block_total = jnp.sum(weights, axis=0, keepdims=True)
            block_out = lax.dot_general(
                value_block,
                weights.astype(jnp.bfloat16),
                (((0,), (0,)), ((), ())),
                preferred_element_type=jnp.float32,
            )
            joined = jnp.maximum(top, block_top)
            older = jnp.exp((top - joined) * scaling)
            newer = jnp.exp((block_top - joined) * scaling)
            out = out * older + block_out * newer
            total = total * older + block_total * newer
            top = joined
        largest = jnp.max(jnp.abs(out), axis=0, keepdims=True) / total
        grid = jnp.maximum(jnp.ceil(largest * SCALE_GRID), 1.0)
        coded = jnp.round(out * (STEPS * SCALE_GRID / (grid * total)))
        log_sum = jnp.maximum(top * scaling + jnp.log(total), LOW)
        whole = jnp.floor(log_sum)
        part = jnp.floor((log_sum - whole) * FINE)
        stats = jnp.concatenate(
            [whole, part, grid, jnp.zeros((STATS - 3, wide), jnp.float32)], axis=0
        )
        message = jnp.concatenate([coded, stats], axis=0).astype(jnp.int32).astype(jnp.int16)
        for at in range(len(steps)):
            out_refs[at][kv] = message[:, at * columns : (at + 1) * columns]


def settle_kernel(*refs, count, rows, kv_heads, group):
    message_refs, out_ref = refs[:count], refs[count]
    width = out_ref.shape[3]
    for kv in range(kv_heads):
        sums, grids = [], []
        for ref in message_refs:
            stats = ref[kv, width : width + STATS].astype(jnp.float32)
            sums.append(stats[0:1] + stats[1:2] * (1.0 / FINE))
            grids.append(stats[2:3])
        highest = functools.reduce(jnp.maximum, sums)
        shares = [jnp.exp(s - highest) for s in sums]
        whole = functools.reduce(jnp.add, shares)
        result = None
        for ref, share, grid in zip(message_refs, shares, grids):
            term = ref[kv, :width].astype(jnp.float32) * (
                share * grid / (whole * (STEPS * SCALE_GRID))
            )
            result = term if result is None else result + term
        result = result.T.reshape(rows, group, width).astype(jnp.bfloat16)
        out_ref[0, :, kv * group : (kv + 1) * group] = result


def per_device(queries, positions, row_order, lengths, cache_keys, cache_values):
    count = lax.axis_size("blk")
    kv_heads, head_dim = cache_keys.shape[1], cache_keys.shape[3]
    rows, heads = queries.shape[1], queries.shape[2]
    group = heads // kv_heads
    tiles = pl.cdiv(count * rows, LANES)
    packed_rows = rows * heads + 16 * tiles
    columns = rows * group
    packed = pl.pallas_call(
        functools.partial(pack_kernel, tiles=tiles),
        out_shape=jax.ShapeDtypeStruct((packed_rows, head_dim), jnp.bfloat16),
        in_specs=[SMEM, SMEM, VMEM],
        out_specs=VMEM,
    )(positions, lengths, queries)
    messages = [packed] + [
        lax.ppermute(packed, "blk", partner_pairs(count, step)) for step in range(1, count)
    ]
    steps = list(range(count))
    parts = pl.pallas_call(
        functools.partial(
            attend_kernel,
            count=count,
            steps=steps,
            rows=rows,
            kv_heads=kv_heads,
            group=group,
            tiles=tiles,
            scaling=float(head_dim) ** -0.5,
        ),
        out_shape=[
            jax.ShapeDtypeStruct((kv_heads, head_dim + STATS, columns), jnp.int16) for _ in steps
        ],
        in_specs=[SMEM, SMEM, VMEM, VMEM] + [VMEM] * count,
        out_specs=[VMEM] * len(steps),
        scratch_shapes=[
            pltpu.VMEM((count, packed_rows, head_dim), jnp.bfloat16),
            pltpu.VMEM((kv_heads, len(steps) * columns, head_dim), jnp.bfloat16),
        ],
        compiler_params=pltpu.CompilerParams(vmem_limit_bytes=32 << 20),
    )(row_order, lengths, cache_keys, cache_values, *messages)
    gathered = [parts[0]] + [
        lax.ppermute(parts[step], "blk", partner_pairs(count, step)) for step in range(1, count)
    ]
    return pl.pallas_call(
        functools.partial(settle_kernel, count=count, rows=rows, kv_heads=kv_heads, group=group),
        out_shape=jax.ShapeDtypeStruct((1, rows, heads, head_dim), jnp.bfloat16),
        in_specs=[VMEM] * count,
        out_specs=VMEM,
    )(*gathered)


def solution(mesh):
    placed = (
        P(("groups", "beam"), "blk", "heads", None),
        P(("groups", "beam"), "blk"),
        P(("groups", "beam"), None),
        P(("groups", "blk")),
        P(("groups", "blk"), "heads", None, None),
        P(("groups", "blk"), "heads", None, None),
    )
    return jax.shard_map(
        per_device,
        mesh=mesh,
        in_specs=placed,
        out_specs=P(("groups", "beam"), "blk", "heads", None),
        check_vma=False,
    )
```

```python
import functools
import math

import jax
import jax.numpy as jnp
from jax import lax
from jax.experimental import pallas as pl
from jax.experimental.pallas import tpu as pltpu
from jax.sharding import PartitionSpec as P

KB = 256
LANES = 128
MASKED = -1e30
LOW = -32768.0
FINE = 32768.0
STEPS = 32767.0
SCALE_GRID = 1024.0
STATS = 16

VMEM = pl.BlockSpec(memory_space=pltpu.VMEM)
SMEM = pl.BlockSpec(memory_space=pltpu.SMEM)
HBM = pl.BlockSpec(memory_space=pltpu.HBM)


def shift_pairs(count, step):
    return [(i, (i + step) % count) for i in range(count)]


def first_source(me, count, step):
    return lax.rem(me - step + count, count)


def second_target(me, count, step):
    return lax.rem(me + step, count)


def in_hbm(*arrays):
    return [pltpu.with_memory_space_constraint(array, pltpu.HBM) for array in arrays]


def pack_kernel(
    lengths_ref, positions_ref, queries_ref, packed_ref, positions, sems, *, tiles
):
    rows, heads, width = queries_ref.shape[1:]
    me = lax.axis_index("blk")
    copies = [
        pltpu.make_async_copy(positions_ref, positions, sems.at[0]),
    ] + [
        pltpu.make_async_copy(
            queries_ref.at[0, row], packed_ref.at[pl.ds(row * heads, heads)], sems.at[1 + row]
        )
        for row in range(rows)
    ]
    for copy in copies:
        copy.start()
    digit = lax.broadcasted_iota(jnp.int32, (16, LANES), 0)
    lane = lax.broadcasted_iota(jnp.int32, (16, LANES), 1)
    copies[0].wait()
    own_length = lengths_ref[0]
    for tile in range(tiles):
        place = lane + tile * LANES
        held = jnp.zeros((16, LANES), jnp.int32)
        for row in range(rows):
            held = jnp.where(place == me * rows + row, positions[0, row], held)
        sized = jnp.where(place == me, own_length, 0)
        digits = jnp.where(digit < 3, held, sized)
        third = jnp.where(digit < 3, digit, digit - 3)
        digits = jnp.where(
            third == 0, digits >> 14, jnp.where(third == 1, (digits >> 7) & 127, digits & 127)
        )
        digits = jnp.where(digit < 6, digits, 0)
        packed_ref[pl.ds(rows * heads + tile * 16, 16)] = digits.astype(jnp.float32).astype(jnp.bfloat16)
    for copy in copies[1:]:
        copy.wait()


def stage_kernel(*refs, count, plan, rows, group):
    keys_ref, values_ref, order_ref = refs[:3]
    keys_out_ref, values_out_ref, order_out_ref, spread_ref = refs[3:7]
    held, order, sems = refs[7:]
    kv_heads, pieces, part = held.shape[:3]
    me = lax.axis_index("blk")
    order_copies = [
        pltpu.make_async_copy(order_ref, order, sems.at[2, 0, 0]),
        pltpu.make_async_copy(order_ref, order_out_ref, sems.at[2, 0, 1]),
    ]
    for copy in order_copies:
        copy.start()
    copies = {}
    for kv in range(kv_heads):
        for piece in range(pieces):
            at = pl.ds(piece * part, part)
            copies[1, kv, piece] = pltpu.make_async_copy(
                values_ref.at[0, kv, at], held.at[kv, piece], sems.at[1, kv, piece]
            )
            copies[0, kv, piece] = pltpu.make_async_copy(
                keys_ref.at[0, kv, at], keys_out_ref.at[kv, at], sems.at[0, kv, piece]
            )
            copies[1, kv, piece].start()
            copies[0, kv, piece].start()
    for copy in order_copies:
        copy.wait()
    columns = rows * group
    lane_row = lax.broadcasted_iota(jnp.int32, (1, columns), 1) // group
    spread_row = lax.broadcasted_iota(jnp.int32, (spread_ref.shape[0], columns), 0)
    for at, step in enumerate(sum(plan, [])):
        chosen = jnp.zeros((1, columns), jnp.int32)
        for i in range(rows):
            chosen = jnp.where(lane_row == i, order[0, second_target(me, count, step) * rows + i], chosen)
        spread = jnp.where(spread_row == chosen, 1.0, 0.0).astype(jnp.bfloat16)
        spread_ref[:, at * columns : (at + 1) * columns] = spread
    for kv in range(kv_heads):
        for piece in range(pieces):
            copies[1, kv, piece].wait()
            values_out_ref[kv, :, piece * part : (piece + 1) * part] = held[kv, piece].T
            copies[0, kv, piece].wait()


def attend(keys_ref, values_ref, asked, counts, out_refs, scores, scaling):
    kv_heads, capacity, wide = scores.shape
    columns = wide // len(out_refs)
    head_dim = values_ref.shape[1]
    slot = lax.broadcasted_iota(jnp.int32, (KB, wide), 0)
    rate = scaling * math.log2(math.e)
    for kv in range(kv_heads):
        scores[kv] = lax.dot_general(
            keys_ref[kv], asked[kv], (((1,), (1,)), ((), ())), preferred_element_type=jnp.float32
        )
    stats = []
    for kv in range(kv_heads):
        tops, totals, outs = [], [], []
        for block in range(capacity // KB):
            at = pl.ds(block * KB, KB)
            seen = jnp.where(slot < counts - block * KB, scores[kv, at], MASKED)
            top = jnp.max(seen, axis=0, keepdims=True)
            weights = jnp.exp2((seen - top) * rate)
            tops.append(top)
            totals.append(jnp.sum(weights, axis=0, keepdims=True))
            outs.append(
                jnp.dot(
                    values_ref[kv, :, at], weights.astype(jnp.bfloat16), preferred_element_type=jnp.float32
                )
            )
        top = functools.reduce(jnp.maximum, tops)
        factors = [jnp.exp2((t - top) * rate) for t in tops]
        total = functools.reduce(jnp.add, [f * t for f, t in zip(factors, totals)])
        out = functools.reduce(jnp.add, [f * o for f, o in zip(factors, outs)])
        largest = jnp.max(jnp.abs(out), axis=0, keepdims=True) / total
        grid = jnp.maximum(jnp.ceil(largest * SCALE_GRID), 1.0)
        coded = jnp.round(out * (STEPS * SCALE_GRID / (grid * total)))
        log_sum = jnp.maximum(top * scaling + jnp.log(total), LOW)
        whole = jnp.floor(log_sum)
        part = jnp.floor((log_sum - whole) * FINE)
        stats += [whole, part, grid]
        coded = coded.astype(jnp.int32).astype(jnp.int16)
        for at, ref in enumerate(out_refs):
            ref[kv * head_dim : (kv + 1) * head_dim] = coded[:, at * columns : (at + 1) * columns]
    spare = out_refs[0].shape[0] - kv_heads * head_dim - len(stats)
    stats = jnp.concatenate(stats + [jnp.zeros((spare, wide), jnp.float32)], axis=0)
    stats = stats.astype(jnp.int32).astype(jnp.int16)
    for at, ref in enumerate(out_refs):
        ref[kv_heads * head_dim :] = stats[:, at * columns : (at + 1) * columns]


def first_kernel(*refs, count, plan, rows, group, scaling):
    order_ref, keys_ref, values_ref, spread_ref = refs[:4]
    message_refs = refs[4 : 4 + count]
    asked_ref, counts_ref = refs[4 + count : 6 + count]
    out_refs, held, scores = refs[6 + count : -2], refs[-2], refs[-1]
    me = lax.axis_index("blk")
    kv_heads, _, wide = scores.shape
    columns = rows * group
    heads = kv_heads * group
    body = held.shape[1]
    tiles = spread_ref.shape[0] // LANES
    for step, ref in zip(first_order(count), message_refs):
        held[first_source(me, count, step)] = ref[:body]
    offset = jnp.zeros((1, 1), jnp.float32)
    own_length = jnp.zeros((1, 1), jnp.float32)
    pos = []
    for tile in range(tiles):
        at = pl.ds(body + tile * 16, 16)
        digits = functools.reduce(jnp.add, [ref[at].astype(jnp.float32) for ref in message_refs])
        pos.append(digits[0:1] * 16384.0 + digits[1:2] * 128.0 + digits[2:3])
        sizes = digits[3:4] * 16384.0 + digits[4:5] * 128.0 + digits[5:6]
        lane = lax.broadcasted_iota(jnp.int32, (1, LANES), 1) + tile * LANES
        offset += jnp.sum(jnp.where(lane < me, sizes, 0.0), axis=1, keepdims=True)
        own_length += jnp.sum(jnp.where(lane == me, sizes, 0.0), axis=1, keepdims=True)
    live = jnp.minimum(jnp.maximum(jnp.concatenate(pos, axis=1) - offset, 0.0), own_length)
    high = jnp.floor(live * (1.0 / 128.0))
    live_digits = jnp.concatenate(
        [high, live - high * 128.0, jnp.zeros((14, tiles * LANES), jnp.float32)], axis=0
    ).astype(jnp.bfloat16)
    both = jnp.dot(live_digits, spread_ref[...], preferred_element_type=jnp.float32)
    counts = (both[0:1] * 128.0 + both[1:2]).astype(jnp.int32)
    counts_ref[...] = jnp.broadcast_to(counts, counts_ref.shape)
    asked = [[] for _ in range(kv_heads)]
    for at, step in enumerate(sum(plan, [])):
        for i in range(rows):
            row = order_ref[0, second_target(me, count, step) * rows + i]
            source = lax.div(row, rows)
            inner = row - source * rows
            for kv in range(kv_heads):
                start = pl.multiple_of(inner * heads + kv * group, group)
                query = held[source, pl.ds(start, group)]
                asked_ref[kv, pl.ds(at * columns + i * group, group)] = query
                if at < len(out_refs):
                    asked[kv].append(query)
    asked = [jnp.concatenate(queries, axis=0) for queries in asked]
    attend(keys_ref, values_ref, asked, counts[:, :wide], out_refs, scores, scaling)


def next_kernel(*refs, start, scaling):
    keys_ref, values_ref, asked_ref, counts_ref = refs[:4]
    out_refs, scores = refs[4:-1], refs[-1]
    kv_heads, _, wide = scores.shape
    asked = [asked_ref[kv, pl.ds(start, wide)] for kv in range(kv_heads)]
    counts = counts_ref[0:1, start : start + wide]
    attend(keys_ref, values_ref, asked, counts, out_refs, scores, scaling)


def settle_kernel(*refs, messages, first, last, kv_heads, width, group):
    message_refs, refs = refs[:messages], refs[messages:]
    if not first:
        out_ref, stat_ref, refs = refs[0], refs[1], refs[2:]
    columns = message_refs[0].shape[1]
    all_stats = [ref[kv_heads * width :].astype(jnp.float32) for ref in message_refs]
    for kv in range(kv_heads):
        sums = [s[3 * kv : 3 * kv + 1] + s[3 * kv + 1 : 3 * kv + 2] * (1.0 / FINE) for s in all_stats]
        grids = [s[3 * kv + 2 : 3 * kv + 3] for s in all_stats]
        tops = sums if first else sums + [stat_ref[kv, 0:1]]
        highest = functools.reduce(jnp.maximum, tops)
        shares = [jnp.exp(s - highest) for s in tops]
        total, result = None, None
        if not first:
            total = shares[-1] * stat_ref[kv, 1:2]
            result = shares[-1] * out_ref[kv]
        for ref, share, grid in zip(message_refs, shares, grids):
            held = ref[kv * width : (kv + 1) * width].astype(jnp.float32)
            term = held * (share * grid * (1.0 / (STEPS * SCALE_GRID)))
            total = share if total is None else total + share
            result = term if result is None else result + term
        if last:
            result = (result / total).T.reshape(columns // group, group, width)
            refs[0][0, :, kv * group : (kv + 1) * group] = result.astype(jnp.bfloat16)
        else:
            refs[0][kv] = result
            refs[1][kv] = jnp.concatenate([highest, total, jnp.zeros((6, columns), jnp.float32)], axis=0)


def first_order(count):
    return [0] + list(reversed(range(1, count)))


STAGE_COST = 16777216
OWN_COST = 1
ATTEND_COST = 1
JOIN_COST = 1


def exchange_plan(count):
    later = sorted(range(1, count), key=lambda step: (abs(2 * step - count), step)) + [0]
    chunk = pl.cdiv(count, 4)
    return [later[i : i + chunk] for i in range(0, count, chunk)]


def join_plan(plan):
    return [plan[-1] + plan[0]] + plan[1:-1]


def cost_of(flops):
    return pl.CostEstimate(flops=int(flops), bytes_accessed=1, transcendentals=0)


def per_device(queries, positions, row_order, lengths, cache_keys, cache_values):
    count = lax.axis_size("blk")
    kv_heads, capacity, head_dim = cache_keys.shape[1:]
    rows, heads = queries.shape[1], queries.shape[2]
    group = heads // kv_heads
    tiles = pl.cdiv(count * rows, LANES)
    body = rows * heads
    columns = rows * group
    scaling = float(head_dim) ** -0.5
    packed = pl.pallas_call(
        functools.partial(pack_kernel, tiles=tiles),
        out_shape=jax.ShapeDtypeStruct((body + 16 * tiles, head_dim), jnp.bfloat16),
        in_specs=[SMEM, HBM, HBM],
        out_specs=VMEM,
        scratch_shapes=[
            pltpu.SMEM(positions.shape, jnp.int32),
            pltpu.SemaphoreType.DMA((1 + rows,)),
        ],
        compiler_params=pltpu.CompilerParams(vmem_limit_bytes=4 << 20),
    )(lengths, *in_hbm(positions, queries))
    arrived = {
        step: lax.ppermute(packed, "blk", shift_pairs(count, step)) for step in range(1, count)
    }

    plan = exchange_plan(count)
    pieces = capacity // KB
    staged_keys, staged_values, order, spread = pl.pallas_call(
        functools.partial(stage_kernel, count=count, plan=plan, rows=rows, group=group),
        out_shape=[
            jax.ShapeDtypeStruct((kv_heads, capacity, head_dim), jnp.bfloat16),
            jax.ShapeDtypeStruct((kv_heads, head_dim, capacity), jnp.bfloat16),
            jax.ShapeDtypeStruct(row_order.shape, jnp.int32),
            jax.ShapeDtypeStruct((tiles * LANES, count * columns), jnp.bfloat16),
        ],
        in_specs=[HBM, HBM, HBM],
        out_specs=[VMEM, VMEM, VMEM, VMEM],
        scratch_shapes=[
            pltpu.VMEM((kv_heads, pieces, KB, head_dim), jnp.bfloat16),
            pltpu.SMEM(row_order.shape, jnp.int32),
            pltpu.SemaphoreType.DMA((3, kv_heads, pieces)),
        ],
        compiler_params=pltpu.CompilerParams(vmem_limit_bytes=8 << 20),
        cost_estimate=cost_of(STAGE_COST),
    )(*in_hbm(cache_keys, cache_values, row_order))

    sent, gathered, start = {}, None, 0
    message_rows = kv_heads * head_dim + 16 * pl.cdiv(3 * kv_heads, 16)
    for steps in plan:
        wide = len(steps) * columns
        shapes = [jax.ShapeDtypeStruct((message_rows, columns), jnp.int16) for _ in steps]
        scores = pltpu.VMEM((kv_heads, capacity, wide), jnp.float32)
        params = pltpu.CompilerParams(vmem_limit_bytes=16 << 20)
        cost = cost_of(OWN_COST if 0 in steps else ATTEND_COST)
        if gathered is None:
            asked, counts, *parts = pl.pallas_call(
                functools.partial(
                    first_kernel, count=count, plan=plan, rows=rows, group=group, scaling=scaling
                ),
                out_shape=[
                    jax.ShapeDtypeStruct((kv_heads, count * columns, head_dim), jnp.bfloat16),
                    jax.ShapeDtypeStruct((8, count * columns), jnp.int32),
                    *shapes,
                ],
                in_specs=[SMEM, VMEM, VMEM, VMEM] + [VMEM] * count,
                out_specs=[VMEM] * (2 + len(steps)),
                scratch_shapes=[pltpu.VMEM((count, body, head_dim), jnp.bfloat16), scores],
                compiler_params=params,
                cost_estimate=cost,
            )(
                order, staged_keys, staged_values, spread,
                *[arrived[s] if s else packed for s in first_order(count)],
            )
            gathered = (asked, counts)
        else:
            parts = pl.pallas_call(
                functools.partial(next_kernel, start=start, scaling=scaling),
                out_shape=shapes,
                in_specs=[VMEM, VMEM, VMEM, VMEM],
                out_specs=[VMEM] * len(steps),
                scratch_shapes=[scores],
                compiler_params=params,
                cost_estimate=cost,
            )(staged_keys, staged_values, *gathered)
        start += wide
        for step, part in zip(steps, parts):
            sent[step] = part if step == 0 else lax.ppermute(part, "blk", shift_pairs(count, step))

    state = []
    joins = join_plan(plan)
    for number, steps in enumerate(joins):
        last = number == len(joins) - 1
        shape = (
            jax.ShapeDtypeStruct((1, rows, heads, head_dim), jnp.bfloat16)
            if last
            else [
                jax.ShapeDtypeStruct((kv_heads, head_dim, columns), jnp.float32),
                jax.ShapeDtypeStruct((kv_heads, 8, columns), jnp.float32),
            ]
        )
        state = pl.pallas_call(
            functools.partial(
                settle_kernel, messages=len(steps), first=not state, last=last,
                kv_heads=kv_heads, width=head_dim, group=group,
            ),
            out_shape=shape,
            in_specs=[VMEM] * (len(steps) + len(state)),
            out_specs=VMEM if last else [VMEM, VMEM],
            compiler_params=pltpu.CompilerParams(vmem_limit_bytes=8 << 20),
            cost_estimate=cost_of(JOIN_COST),
        )(*[sent[step] for step in steps], *state)
    return state


def solution(mesh):
    placed = (
        P(("groups", "beam"), "blk", "heads", None),
        P(("groups", "beam"), "blk"),
        P(("groups", "beam"), None),
        P(("groups", "blk")),
        P(("groups", "blk"), "heads", None, None),
        P(("groups", "blk"), "heads", None, None),
    )
    return jax.shard_map(
        per_device,
        mesh=mesh,
        in_specs=placed,
        out_specs=P(("groups", "beam"), "blk", "heads", None),
        check_vma=False,
    )
```

```python
import functools
import math

import jax
import jax.numpy as jnp
from jax import lax
from jax.experimental import pallas as pl
from jax.experimental.pallas import tpu as pltpu
from jax.sharding import PartitionSpec as P

KB = 256
LANES = 128
MASKED = -1e30
LOW = -32768.0
FINE = 32768.0
STEPS = 32767.0
SCALE_GRID = 1024.0
STATS = 16

VMEM = pl.BlockSpec(memory_space=pltpu.VMEM)
SMEM = pl.BlockSpec(memory_space=pltpu.SMEM)
HBM = pl.BlockSpec(memory_space=pltpu.HBM)


def shift_pairs(count, step):
    return [(i, (i + step) % count) for i in range(count)]


def shift_source(me, count, step):
    return lax.rem(me - step + count, count)


def shift_target(me, count, step):
    return lax.rem(me + step, count)


def in_hbm(*arrays):
    return [pltpu.with_memory_space_constraint(array, pltpu.HBM) for array in arrays]


def pack_kernel(
    lengths_ref, positions_ref, queries_ref, packed_ref, positions, sems, *, tiles
):
    rows, heads, width = queries_ref.shape[1:]
    me = lax.axis_index("blk")
    copies = [
        pltpu.make_async_copy(positions_ref, positions, sems.at[0]),
    ] + [
        pltpu.make_async_copy(
            queries_ref.at[0, row], packed_ref.at[pl.ds(row * heads, heads)], sems.at[1 + row]
        )
        for row in range(rows)
    ]
    for copy in copies:
        copy.start()
    digit = lax.broadcasted_iota(jnp.int32, (16, LANES), 0)
    lane = lax.broadcasted_iota(jnp.int32, (16, LANES), 1)
    copies[0].wait()
    own_length = lengths_ref[0]
    for tile in range(tiles):
        place = lane + tile * LANES
        held = jnp.zeros((16, LANES), jnp.int32)
        for row in range(rows):
            held = jnp.where(place == me * rows + row, positions[0, row], held)
        sized = jnp.where(place == me, own_length, 0)
        digits = jnp.where(digit < 3, held, sized)
        third = jnp.where(digit < 3, digit, digit - 3)
        digits = jnp.where(
            third == 0, digits >> 14, jnp.where(third == 1, (digits >> 7) & 127, digits & 127)
        )
        digits = jnp.where(digit < 6, digits, 0)
        packed_ref[pl.ds(rows * heads + tile * 16, 16)] = digits.astype(jnp.float32).astype(jnp.bfloat16)
    for copy in copies[1:]:
        copy.wait()


def stage_kernel(*refs, count, plan, rows, group):
    keys_ref, values_ref, order_ref = refs[:3]
    keys_out_ref, values_out_ref, order_out_ref, spread_ref = refs[3:7]
    held, order, sems = refs[7:]
    kv_heads, pieces, part = held.shape[:3]
    me = lax.axis_index("blk")
    order_copies = [
        pltpu.make_async_copy(order_ref, order, sems.at[2, 0, 0]),
        pltpu.make_async_copy(order_ref, order_out_ref, sems.at[2, 0, 1]),
    ]
    for copy in order_copies:
        copy.start()
    copies = {}
    for kv in range(kv_heads):
        for piece in range(pieces):
            at = pl.ds(piece * part, part)
            copies[1, kv, piece] = pltpu.make_async_copy(
                values_ref.at[0, kv, at], held.at[kv, piece], sems.at[1, kv, piece]
            )
            copies[0, kv, piece] = pltpu.make_async_copy(
                keys_ref.at[0, kv, at], keys_out_ref.at[kv, at], sems.at[0, kv, piece]
            )
            copies[1, kv, piece].start()
            copies[0, kv, piece].start()
    for copy in order_copies:
        copy.wait()
    columns = rows * group
    lane_row = lax.broadcasted_iota(jnp.int32, (1, columns), 1) // group
    spread_row = lax.broadcasted_iota(jnp.int32, (spread_ref.shape[0], columns), 0)
    for at, step in enumerate(sum(plan, [])):
        chosen = jnp.zeros((1, columns), jnp.int32)
        for i in range(rows):
            chosen = jnp.where(lane_row == i, order[0, shift_target(me, count, step) * rows + i], chosen)
        spread = jnp.where(spread_row == chosen, 1.0, 0.0).astype(jnp.bfloat16)
        spread_ref[:, at * columns : (at + 1) * columns] = spread
    for kv in range(kv_heads):
        for piece in range(pieces):
            copies[1, kv, piece].wait()
            values_out_ref[kv, :, piece * part : (piece + 1) * part] = held[kv, piece].T
            copies[0, kv, piece].wait()


def attend(keys_ref, values_ref, asked, counts, out_refs, scores, scaling):
    kv_heads, capacity, wide = scores.shape
    columns = wide // len(out_refs)
    head_dim = values_ref.shape[1]
    slot = lax.broadcasted_iota(jnp.int32, (KB, wide), 0)
    rate = scaling * math.log2(math.e)
    for kv in range(kv_heads):
        scores[kv] = lax.dot_general(
            keys_ref[kv], asked[kv], (((1,), (1,)), ((), ())), preferred_element_type=jnp.float32
        )
    stats = []
    for kv in range(kv_heads):
        tops, totals, outs = [], [], []
        for block in range(capacity // KB):
            at = pl.ds(block * KB, KB)
            seen = jnp.where(slot < counts - block * KB, scores[kv, at], MASKED)
            top = jnp.max(seen, axis=0, keepdims=True)
            weights = jnp.exp2((seen - top) * rate)
            tops.append(top)
            totals.append(jnp.sum(weights, axis=0, keepdims=True))
            outs.append(
                jnp.dot(
                    values_ref[kv, :, at], weights.astype(jnp.bfloat16), preferred_element_type=jnp.float32
                )
            )
        top = functools.reduce(jnp.maximum, tops)
        factors = [jnp.exp2((t - top) * rate) for t in tops]
        total = functools.reduce(jnp.add, [f * t for f, t in zip(factors, totals)])
        out = functools.reduce(jnp.add, [f * o for f, o in zip(factors, outs)])
        largest = jnp.max(jnp.abs(out), axis=0, keepdims=True) / total
        grid = jnp.maximum(jnp.ceil(largest * SCALE_GRID), 1.0)
        coded = jnp.round(out * (STEPS * SCALE_GRID / (grid * total)))
        log_sum = jnp.maximum(top * scaling + jnp.log(total), LOW)
        whole = jnp.floor(log_sum)
        part = jnp.floor((log_sum - whole) * FINE)
        stats += [whole, part, grid]
        coded = coded.astype(jnp.int32).astype(jnp.int16)
        for at, ref in enumerate(out_refs):
            ref[kv * head_dim : (kv + 1) * head_dim] = coded[:, at * columns : (at + 1) * columns]
    spare = out_refs[0].shape[0] - kv_heads * head_dim - len(stats)
    stats = jnp.concatenate(stats + [jnp.zeros((spare, wide), jnp.float32)], axis=0)
    stats = stats.astype(jnp.int32).astype(jnp.int16)
    for at, ref in enumerate(out_refs):
        ref[kv_heads * head_dim :] = stats[:, at * columns : (at + 1) * columns]


def first_kernel(*refs, count, plan, rows, group, scaling):
    order_ref, keys_ref, values_ref, spread_ref = refs[:4]
    message_refs = refs[4 : 4 + count]
    asked_ref, counts_ref = refs[4 + count : 6 + count]
    out_refs, held, scores = refs[6 + count : -2], refs[-2], refs[-1]
    me = lax.axis_index("blk")
    kv_heads, _, wide = scores.shape
    columns = rows * group
    heads = kv_heads * group
    body = held.shape[1]
    tiles = spread_ref.shape[0] // LANES
    for step, ref in zip(first_order(count), message_refs):
        held[shift_source(me, count, step)] = ref[:body]
    offset = jnp.zeros((1, 1), jnp.float32)
    own_length = jnp.zeros((1, 1), jnp.float32)
    pos = []
    for tile in range(tiles):
        at = pl.ds(body + tile * 16, 16)
        digits = functools.reduce(jnp.add, [ref[at].astype(jnp.float32) for ref in message_refs])
        pos.append(digits[0:1] * 16384.0 + digits[1:2] * 128.0 + digits[2:3])
        sizes = digits[3:4] * 16384.0 + digits[4:5] * 128.0 + digits[5:6]
        lane = lax.broadcasted_iota(jnp.int32, (1, LANES), 1) + tile * LANES
        offset += jnp.sum(jnp.where(lane < me, sizes, 0.0), axis=1, keepdims=True)
        own_length += jnp.sum(jnp.where(lane == me, sizes, 0.0), axis=1, keepdims=True)
    live = jnp.minimum(jnp.maximum(jnp.concatenate(pos, axis=1) - offset, 0.0), own_length)
    high = jnp.floor(live * (1.0 / 128.0))
    live_digits = jnp.concatenate(
        [high, live - high * 128.0, jnp.zeros((14, tiles * LANES), jnp.float32)], axis=0
    ).astype(jnp.bfloat16)
    both = jnp.dot(live_digits, spread_ref[...], preferred_element_type=jnp.float32)
    counts = (both[0:1] * 128.0 + both[1:2]).astype(jnp.int32)
    counts_ref[...] = jnp.broadcast_to(counts, counts_ref.shape)
    asked = [[] for _ in range(kv_heads)]
    for at, step in enumerate(sum(plan, [])):
        for i in range(rows):
            row = order_ref[0, shift_target(me, count, step) * rows + i]
            source = lax.div(row, rows)
            inner = row - source * rows
            for kv in range(kv_heads):
                start = pl.multiple_of(inner * heads + kv * group, group)
                query = held[source, pl.ds(start, group)]
                asked_ref[kv, pl.ds(at * columns + i * group, group)] = query
                if at < len(out_refs):
                    asked[kv].append(query)
    asked = [jnp.concatenate(queries, axis=0) for queries in asked]
    attend(keys_ref, values_ref, asked, counts[:, :wide], out_refs, scores, scaling)


def next_kernel(*refs, start, scaling):
    keys_ref, values_ref, asked_ref, counts_ref = refs[:4]
    out_refs, scores = refs[4:-1], refs[-1]
    kv_heads, _, wide = scores.shape
    asked = [asked_ref[kv, pl.ds(start, wide)] for kv in range(kv_heads)]
    counts = counts_ref[0:1, start : start + wide]
    attend(keys_ref, values_ref, asked, counts, out_refs, scores, scaling)


def settle_kernel(*refs, messages, first, last, kv_heads, width, group):
    message_refs, refs = refs[:messages], refs[messages:]
    if not first:
        out_ref, stat_ref, refs = refs[0], refs[1], refs[2:]
    columns = message_refs[0].shape[1]
    all_stats = [ref[kv_heads * width :].astype(jnp.float32) for ref in message_refs]
    for kv in range(kv_heads):
        sums = [s[3 * kv : 3 * kv + 1] + s[3 * kv + 1 : 3 * kv + 2] * (1.0 / FINE) for s in all_stats]
        grids = [s[3 * kv + 2 : 3 * kv + 3] for s in all_stats]
        tops = sums if first else sums + [stat_ref[kv, 0:1]]
        highest = functools.reduce(jnp.maximum, tops)
        shares = [jnp.exp(s - highest) for s in tops]
        total, result = None, None
        if not first:
            total = shares[-1] * stat_ref[kv, 1:2]
            result = shares[-1] * out_ref[kv]
        for ref, share, grid in zip(message_refs, shares, grids):
            held = ref[kv * width : (kv + 1) * width].astype(jnp.float32)
            term = held * (share * grid * (1.0 / (STEPS * SCALE_GRID)))
            total = share if total is None else total + share
            result = term if result is None else result + term
        if last:
            result = (result / total).T.reshape(columns // group, group, width)
            refs[0][0, :, kv * group : (kv + 1) * group] = result.astype(jnp.bfloat16)
        else:
            refs[0][kv] = result
            refs[1][kv] = jnp.concatenate([highest, total, jnp.zeros((6, columns), jnp.float32)], axis=0)


def first_order(count):
    return [0] + list(reversed(range(1, count)))


STAGE_COST = 16777216
OWN_COST = 1
ATTEND_COST = 1
JOIN_COST = 1


def exchange_plan(count):
    later = sorted(range(1, count), key=lambda step: (abs(2 * step - count), step))
    chunk = pl.cdiv(count, 4)
    rest = later[chunk:]
    pairs = [rest[i : i + 2 * chunk] for i in range(0, len(rest), 2 * chunk)]
    return [later[:chunk], *pairs, [0]]


def join_plan(plan):
    chunk = len(plan[0])
    rest = sum(plan[1:-1], [])
    return [plan[-1] + plan[0]] + [rest[i : i + chunk] for i in range(0, len(rest), chunk)]


def cost_of(flops):
    return pl.CostEstimate(flops=int(flops), bytes_accessed=1, transcendentals=0)


def per_device(queries, positions, row_order, lengths, cache_keys, cache_values):
    count = lax.axis_size("blk")
    kv_heads, capacity, head_dim = cache_keys.shape[1:]
    rows, heads = queries.shape[1], queries.shape[2]
    group = heads // kv_heads
    tiles = pl.cdiv(count * rows, LANES)
    body = rows * heads
    columns = rows * group
    scaling = float(head_dim) ** -0.5
    packed = pl.pallas_call(
        functools.partial(pack_kernel, tiles=tiles),
        out_shape=jax.ShapeDtypeStruct((body + 16 * tiles, head_dim), jnp.bfloat16),
        in_specs=[SMEM, HBM, HBM],
        out_specs=VMEM,
        scratch_shapes=[
            pltpu.SMEM(positions.shape, jnp.int32),
            pltpu.SemaphoreType.DMA((1 + rows,)),
        ],
        compiler_params=pltpu.CompilerParams(vmem_limit_bytes=4 << 20),
    )(lengths, *in_hbm(positions, queries))
    arrived = {
        step: lax.ppermute(packed, "blk", shift_pairs(count, step)) for step in range(1, count)
    }

    plan = exchange_plan(count)
    pieces = capacity // KB
    staged_keys, staged_values, order, spread = pl.pallas_call(
        functools.partial(stage_kernel, count=count, plan=plan, rows=rows, group=group),
        out_shape=[
            jax.ShapeDtypeStruct((kv_heads, capacity, head_dim), jnp.bfloat16),
            jax.ShapeDtypeStruct((kv_heads, head_dim, capacity), jnp.bfloat16),
            pltpu.SMEM(row_order.shape, jnp.int32),
            jax.ShapeDtypeStruct((tiles * LANES, count * columns), jnp.bfloat16),
        ],
        in_specs=[HBM, HBM, HBM],
        out_specs=[VMEM, VMEM, SMEM, VMEM],
        scratch_shapes=[
            pltpu.VMEM((kv_heads, pieces, KB, head_dim), jnp.bfloat16),
            pltpu.SMEM(row_order.shape, jnp.int32),
            pltpu.SemaphoreType.DMA((3, kv_heads, pieces)),
        ],
        compiler_params=pltpu.CompilerParams(vmem_limit_bytes=8 << 20),
        cost_estimate=cost_of(STAGE_COST),
    )(*in_hbm(cache_keys, cache_values, row_order))

    sent, gathered, start = {}, None, 0
    message_rows = kv_heads * head_dim + 16 * pl.cdiv(3 * kv_heads, 16)
    for steps in plan:
        wide = len(steps) * columns
        shapes = [jax.ShapeDtypeStruct((message_rows, columns), jnp.int16) for _ in steps]
        scores = pltpu.VMEM((kv_heads, capacity, wide), jnp.float32)
        params = pltpu.CompilerParams(vmem_limit_bytes=16 << 20)
        cost = cost_of(OWN_COST if 0 in steps else ATTEND_COST)
        if gathered is None:
            asked, counts, *parts = pl.pallas_call(
                functools.partial(
                    first_kernel, count=count, plan=plan, rows=rows, group=group, scaling=scaling
                ),
                out_shape=[
                    jax.ShapeDtypeStruct((kv_heads, count * columns, head_dim), jnp.bfloat16),
                    jax.ShapeDtypeStruct((8, count * columns), jnp.int32),
                    *shapes,
                ],
                in_specs=[SMEM, VMEM, VMEM, VMEM] + [VMEM] * count,
                out_specs=[VMEM] * (2 + len(steps)),
                scratch_shapes=[pltpu.VMEM((count, body, head_dim), jnp.bfloat16), scores],
                compiler_params=params,
                cost_estimate=cost,
            )(
                order, staged_keys, staged_values, spread,
                *[arrived[s] if s else packed for s in first_order(count)],
            )
            gathered = (asked, counts)
        else:
            parts = pl.pallas_call(
                functools.partial(next_kernel, start=start, scaling=scaling),
                out_shape=shapes,
                in_specs=[VMEM, VMEM, VMEM, VMEM],
                out_specs=[VMEM] * len(steps),
                scratch_shapes=[scores],
                compiler_params=params,
                cost_estimate=cost,
            )(staged_keys, staged_values, *gathered)
        start += wide
        for step, part in zip(steps, parts):
            sent[step] = part if step == 0 else lax.ppermute(part, "blk", shift_pairs(count, step))

    state = []
    joins = join_plan(plan)
    for number, steps in enumerate(joins):
        last = number == len(joins) - 1
        shape = (
            jax.ShapeDtypeStruct((1, rows, heads, head_dim), jnp.bfloat16)
            if last
            else [
                jax.ShapeDtypeStruct((kv_heads, head_dim, columns), jnp.float32),
                jax.ShapeDtypeStruct((kv_heads, 8, columns), jnp.float32),
            ]
        )
        state = pl.pallas_call(
            functools.partial(
                settle_kernel, messages=len(steps), first=not state, last=last,
                kv_heads=kv_heads, width=head_dim, group=group,
            ),
            out_shape=shape,
            in_specs=[VMEM] * (len(steps) + len(state)),
            out_specs=VMEM if last else [VMEM, VMEM],
            compiler_params=pltpu.CompilerParams(vmem_limit_bytes=8 << 20),
            cost_estimate=cost_of(JOIN_COST),
        )(*[sent[step] for step in steps], *state)
    return state


def solution(mesh):
    placed = (
        P(("groups", "beam"), "blk", "heads", None),
        P(("groups", "beam"), "blk"),
        P(("groups", "beam"), None),
        P(("groups", "blk")),
        P(("groups", "blk"), "heads", None, None),
        P(("groups", "blk"), "heads", None, None),
    )
    return jax.shard_map(
        per_device,
        mesh=mesh,
        in_specs=placed,
        out_specs=P(("groups", "beam"), "blk", "heads", None),
        check_vma=False,
    )
```

```python
import functools
import math

import jax
import jax.numpy as jnp
from jax import lax
from jax.experimental import pallas as pl
from jax.experimental.pallas import tpu as pltpu
from jax.sharding import PartitionSpec as P

KB = 256
LANES = 128
MASKED = -1e30
LOW = -32768.0
FINE = 32768.0
STEPS = 32767.0
SCALE_GRID = 1024.0
STATS = 16

VMEM = pl.BlockSpec(memory_space=pltpu.VMEM)
SMEM = pl.BlockSpec(memory_space=pltpu.SMEM)
HBM = pl.BlockSpec(memory_space=pltpu.HBM)


def shift_pairs(count, step):
    return [(i, (i + step) % count) for i in range(count)]


def shift_source(me, count, step):
    return lax.rem(me - step + count, count)


def shift_target(me, count, step):
    return lax.rem(me + step, count)


def in_hbm(*arrays):
    return [pltpu.with_memory_space_constraint(array, pltpu.HBM) for array in arrays]


def pack_kernel(
    lengths_ref, positions_ref, queries_ref, packed_ref, positions, sems, *, tiles
):
    rows, heads, width = queries_ref.shape[1:]
    me = lax.axis_index("blk")
    copies = [
        pltpu.make_async_copy(positions_ref, positions, sems.at[0]),
    ] + [
        pltpu.make_async_copy(
            queries_ref.at[0, row], packed_ref.at[pl.ds(row * heads, heads)], sems.at[1 + row]
        )
        for row in range(rows)
    ]
    for copy in copies:
        copy.start()
    digit = lax.broadcasted_iota(jnp.int32, (16, LANES), 0)
    lane = lax.broadcasted_iota(jnp.int32, (16, LANES), 1)
    copies[0].wait()
    own_length = lengths_ref[0]
    for tile in range(tiles):
        place = lane + tile * LANES
        held = jnp.zeros((16, LANES), jnp.int32)
        for row in range(rows):
            held = jnp.where(place == me * rows + row, positions[0, row], held)
        sized = jnp.where(place == me, own_length, 0)
        digits = jnp.where(digit < 3, held, sized)
        third = jnp.where(digit < 3, digit, digit - 3)
        digits = jnp.where(
            third == 0, digits >> 14, jnp.where(third == 1, (digits >> 7) & 127, digits & 127)
        )
        digits = jnp.where(digit < 6, digits, 0)
        packed_ref[pl.ds(rows * heads + tile * 16, 16)] = digits.astype(jnp.float32).astype(jnp.bfloat16)
    for copy in copies[1:]:
        copy.wait()


def stage_kernel(*refs, count, plan, rows, group):
    keys_ref, values_ref, order_ref = refs[:3]
    keys_out_ref, values_out_ref, order_out_ref, spread_ref = refs[3:7]
    held, order, sems = refs[7:]
    kv_heads, pieces, part = held.shape[:3]
    me = lax.axis_index("blk")
    order_copies = [
        pltpu.make_async_copy(order_ref, order, sems.at[2, 0, 0]),
        pltpu.make_async_copy(order_ref, order_out_ref, sems.at[2, 0, 1]),
    ]
    for copy in order_copies:
        copy.start()
    copies = {}
    for kv in range(kv_heads):
        for piece in range(pieces):
            at = pl.ds(piece * part, part)
            copies[1, kv, piece] = pltpu.make_async_copy(
                values_ref.at[0, kv, at], held.at[kv, piece], sems.at[1, kv, piece]
            )
            copies[0, kv, piece] = pltpu.make_async_copy(
                keys_ref.at[0, kv, at], keys_out_ref.at[kv, at], sems.at[0, kv, piece]
            )
            copies[1, kv, piece].start()
            copies[0, kv, piece].start()
    for copy in order_copies:
        copy.wait()
    columns = rows * group
    lane_row = lax.broadcasted_iota(jnp.int32, (1, columns), 1) // group
    spread_row = lax.broadcasted_iota(jnp.int32, (spread_ref.shape[0], columns), 0)
    for at, step in enumerate(sum(plan, [])):
        chosen = jnp.zeros((1, columns), jnp.int32)
        for i in range(rows):
            chosen = jnp.where(lane_row == i, order[0, shift_target(me, count, step) * rows + i], chosen)
        spread = jnp.where(spread_row == chosen, 1.0, 0.0).astype(jnp.bfloat16)
        spread_ref[:, at * columns : (at + 1) * columns] = spread
    for kv in range(kv_heads):
        for piece in range(pieces):
            copies[1, kv, piece].wait()
            values_out_ref[kv, :, piece * part : (piece + 1) * part] = held[kv, piece].T
            copies[0, kv, piece].wait()


def attend(keys_ref, values_ref, asked, counts, out_refs, scores, scaling, blocks):
    kv_heads, _, wide = scores.shape
    columns = wide // len(out_refs)
    head_dim = values_ref.shape[1]
    slot = lax.broadcasted_iota(jnp.int32, (KB, wide), 0)
    rate = scaling * math.log2(math.e)
    for kv in range(kv_heads):
        scores[kv, : blocks * KB] = lax.dot_general(
            keys_ref[kv, : blocks * KB], asked[kv], (((1,), (1,)), ((), ())), preferred_element_type=jnp.float32
        )
    stats = []
    for kv in range(kv_heads):
        tops, totals, outs = [], [], []
        for block in range(blocks):
            at = pl.ds(block * KB, KB)
            seen = jnp.where(slot < counts - block * KB, scores[kv, at], MASKED)
            top = jnp.max(seen, axis=0, keepdims=True)
            weights = jnp.exp2((seen - top) * rate)
            tops.append(top)
            totals.append(jnp.sum(weights, axis=0, keepdims=True))
            outs.append(
                jnp.dot(
                    values_ref[kv, :, at], weights.astype(jnp.bfloat16), preferred_element_type=jnp.float32
                )
            )
        top = functools.reduce(jnp.maximum, tops)
        factors = [jnp.exp2((t - top) * rate) for t in tops]
        total = functools.reduce(jnp.add, [f * t for f, t in zip(factors, totals)])
        out = functools.reduce(jnp.add, [f * o for f, o in zip(factors, outs)])
        largest = jnp.max(jnp.abs(out), axis=0, keepdims=True) / total
        grid = jnp.maximum(jnp.ceil(largest * SCALE_GRID), 1.0)
        coded = jnp.round(out * (STEPS * SCALE_GRID / (grid * total)))
        log_sum = jnp.maximum(top * scaling + jnp.log(total), LOW)
        whole = jnp.floor(log_sum)
        part = jnp.floor((log_sum - whole) * FINE)
        stats += [whole, part, grid]
        coded = coded.astype(jnp.int32).astype(jnp.int16)
        for at, ref in enumerate(out_refs):
            ref[kv * head_dim : (kv + 1) * head_dim] = coded[:, at * columns : (at + 1) * columns]
    spare = out_refs[0].shape[0] - kv_heads * head_dim - len(stats)
    stats = jnp.concatenate(stats + [jnp.zeros((spare, wide), jnp.float32)], axis=0)
    stats = stats.astype(jnp.int32).astype(jnp.int16)
    for at, ref in enumerate(out_refs):
        ref[kv_heads * head_dim :] = stats[:, at * columns : (at + 1) * columns]


def by_live_blocks(lengths_ref, capacity, body):
    live = lax.div(lengths_ref[0] + (KB - 1), KB)
    most = capacity // KB
    live = jnp.minimum(jnp.maximum(live, 1), most)
    for blocks in range(1, most + 1):
        pl.when(live == blocks)(functools.partial(body, blocks))


def first_kernel(lengths_ref, *refs, count, plan, rows, group, scaling):
    by_live_blocks(
        lengths_ref,
        refs[1].shape[1],
        lambda blocks: first_body(
            *refs, count=count, plan=plan, rows=rows, group=group, scaling=scaling, blocks=blocks
        ),
    )


def first_body(*refs, count, plan, rows, group, scaling, blocks):
    order_ref, keys_ref, values_ref, spread_ref = refs[:4]
    message_refs = refs[4 : 4 + count]
    asked_ref, counts_ref = refs[4 + count : 6 + count]
    out_refs, held, scores = refs[6 + count : -2], refs[-2], refs[-1]
    me = lax.axis_index("blk")
    kv_heads, _, wide = scores.shape
    columns = rows * group
    heads = kv_heads * group
    body = held.shape[1]
    tiles = spread_ref.shape[0] // LANES
    for step, ref in zip(first_order(count), message_refs):
        held[shift_source(me, count, step)] = ref[:body]
    offset = jnp.zeros((1, 1), jnp.float32)
    own_length = jnp.zeros((1, 1), jnp.float32)
    pos = []
    for tile in range(tiles):
        at = pl.ds(body + tile * 16, 16)
        digits = functools.reduce(jnp.add, [ref[at].astype(jnp.float32) for ref in message_refs])
        pos.append(digits[0:1] * 16384.0 + digits[1:2] * 128.0 + digits[2:3])
        sizes = digits[3:4] * 16384.0 + digits[4:5] * 128.0 + digits[5:6]
        lane = lax.broadcasted_iota(jnp.int32, (1, LANES), 1) + tile * LANES
        offset += jnp.sum(jnp.where(lane < me, sizes, 0.0), axis=1, keepdims=True)
        own_length += jnp.sum(jnp.where(lane == me, sizes, 0.0), axis=1, keepdims=True)
    live = jnp.minimum(jnp.maximum(jnp.concatenate(pos, axis=1) - offset, 0.0), own_length)
    high = jnp.floor(live * (1.0 / 128.0))
    live_digits = jnp.concatenate(
        [high, live - high * 128.0, jnp.zeros((14, tiles * LANES), jnp.float32)], axis=0
    ).astype(jnp.bfloat16)
    both = jnp.dot(live_digits, spread_ref[...], preferred_element_type=jnp.float32)
    counts = (both[0:1] * 128.0 + both[1:2]).astype(jnp.int32)
    counts_ref[...] = jnp.broadcast_to(counts, counts_ref.shape)
    asked = [[] for _ in range(kv_heads)]
    for at, step in enumerate(sum(plan, [])):
        for i in range(rows):
            row = order_ref[0, shift_target(me, count, step) * rows + i]
            source = lax.div(row, rows)
            inner = row - source * rows
            for kv in range(kv_heads):
                start = pl.multiple_of(inner * heads + kv * group, group)
                query = held[source, pl.ds(start, group)]
                asked_ref[kv, pl.ds(at * columns + i * group, group)] = query
                if at < len(out_refs):
                    asked[kv].append(query)
    asked = [jnp.concatenate(queries, axis=0) for queries in asked]
    attend(keys_ref, values_ref, asked, counts[:, :wide], out_refs, scores, scaling, blocks)


def next_kernel(lengths_ref, *refs, start, scaling):
    keys_ref, values_ref, asked_ref, counts_ref = refs[:4]
    out_refs, scores = refs[4:-1], refs[-1]
    kv_heads, _, wide = scores.shape

    def body(blocks):
        asked = [asked_ref[kv, pl.ds(start, wide)] for kv in range(kv_heads)]
        counts = counts_ref[0:1, start : start + wide]
        attend(keys_ref, values_ref, asked, counts, out_refs, scores, scaling, blocks)

    by_live_blocks(lengths_ref, keys_ref.shape[1], body)


def settle_kernel(*refs, messages, first, last, kv_heads, width, group):
    message_refs, refs = refs[:messages], refs[messages:]
    if not first:
        out_ref, stat_ref, refs = refs[0], refs[1], refs[2:]
    columns = message_refs[0].shape[1]
    all_stats = [ref[kv_heads * width :].astype(jnp.float32) for ref in message_refs]
    for kv in range(kv_heads):
        sums = [s[3 * kv : 3 * kv + 1] + s[3 * kv + 1 : 3 * kv + 2] * (1.0 / FINE) for s in all_stats]
        grids = [s[3 * kv + 2 : 3 * kv + 3] for s in all_stats]
        tops = sums if first else sums + [stat_ref[kv, 0:1]]
        highest = functools.reduce(jnp.maximum, tops)
        shares = [jnp.exp(s - highest) for s in tops]
        total, result = None, None
        if not first:
            total = shares[-1] * stat_ref[kv, 1:2]
            result = shares[-1] * out_ref[kv]
        for ref, share, grid in zip(message_refs, shares, grids):
            held = ref[kv * width : (kv + 1) * width].astype(jnp.float32)
            term = held * (share * grid * (1.0 / (STEPS * SCALE_GRID)))
            total = share if total is None else total + share
            result = term if result is None else result + term
        if last:
            result = (result / total).T.reshape(columns // group, group, width)
            refs[0][0, :, kv * group : (kv + 1) * group] = result.astype(jnp.bfloat16)
        else:
            refs[0][kv] = result
            refs[1][kv] = jnp.concatenate([highest, total, jnp.zeros((6, columns), jnp.float32)], axis=0)


def first_order(count):
    return [0] + list(reversed(range(1, count)))


STAGE_COST = 16777216
OWN_COST = 1
ATTEND_COST = 1
JOIN_COST = 1


def exchange_plan(count):
    later = sorted(range(1, count), key=lambda step: (abs(2 * step - count), step))
    chunk = pl.cdiv(count, 4)
    rest = later[chunk:]
    pairs = [rest[i : i + 2 * chunk] for i in range(0, len(rest), 2 * chunk)]
    return [later[:chunk], *pairs, [0]]


def join_plan(plan):
    chunk = len(plan[0])
    rest = sum(plan[1:-1], [])
    return [plan[-1] + plan[0]] + [rest[i : i + chunk] for i in range(0, len(rest), chunk)]


def cost_of(flops):
    return pl.CostEstimate(flops=int(flops), bytes_accessed=1, transcendentals=0)


def per_device(queries, positions, row_order, lengths, cache_keys, cache_values):
    count = lax.axis_size("blk")
    kv_heads, capacity, head_dim = cache_keys.shape[1:]
    rows, heads = queries.shape[1], queries.shape[2]
    group = heads // kv_heads
    tiles = pl.cdiv(count * rows, LANES)
    body = rows * heads
    columns = rows * group
    scaling = float(head_dim) ** -0.5
    packed = pl.pallas_call(
        functools.partial(pack_kernel, tiles=tiles),
        out_shape=jax.ShapeDtypeStruct((body + 16 * tiles, head_dim), jnp.bfloat16),
        in_specs=[SMEM, HBM, HBM],
        out_specs=VMEM,
        scratch_shapes=[
            pltpu.SMEM(positions.shape, jnp.int32),
            pltpu.SemaphoreType.DMA((1 + rows,)),
        ],
        compiler_params=pltpu.CompilerParams(vmem_limit_bytes=4 << 20),
    )(lengths, *in_hbm(positions, queries))
    arrived = {
        step: lax.ppermute(packed, "blk", shift_pairs(count, step)) for step in range(1, count)
    }

    plan = exchange_plan(count)
    pieces = capacity // KB
    staged_keys, staged_values, order, spread = pl.pallas_call(
        functools.partial(stage_kernel, count=count, plan=plan, rows=rows, group=group),
        out_shape=[
            jax.ShapeDtypeStruct((kv_heads, capacity, head_dim), jnp.bfloat16),
            jax.ShapeDtypeStruct((kv_heads, head_dim, capacity), jnp.bfloat16),
            pltpu.SMEM(row_order.shape, jnp.int32),
            jax.ShapeDtypeStruct((tiles * LANES, count * columns), jnp.bfloat16),
        ],
        in_specs=[HBM, HBM, HBM],
        out_specs=[VMEM, VMEM, SMEM, VMEM],
        scratch_shapes=[
            pltpu.VMEM((kv_heads, pieces, KB, head_dim), jnp.bfloat16),
            pltpu.SMEM(row_order.shape, jnp.int32),
            pltpu.SemaphoreType.DMA((3, kv_heads, pieces)),
        ],
        compiler_params=pltpu.CompilerParams(vmem_limit_bytes=8 << 20),
        cost_estimate=cost_of(STAGE_COST),
    )(*in_hbm(cache_keys, cache_values, row_order))

    sent, gathered, start = {}, None, 0
    message_rows = kv_heads * head_dim + 16 * pl.cdiv(3 * kv_heads, 16)
    for steps in plan:
        wide = len(steps) * columns
        shapes = [jax.ShapeDtypeStruct((message_rows, columns), jnp.int16) for _ in steps]
        scores = pltpu.VMEM((kv_heads, capacity, wide), jnp.float32)
        params = pltpu.CompilerParams(vmem_limit_bytes=16 << 20)
        cost = cost_of(OWN_COST if 0 in steps else ATTEND_COST)
        if gathered is None:
            asked, counts, *parts = pl.pallas_call(
                functools.partial(
                    first_kernel, count=count, plan=plan, rows=rows, group=group, scaling=scaling
                ),
                out_shape=[
                    jax.ShapeDtypeStruct((kv_heads, count * columns, head_dim), jnp.bfloat16),
                    jax.ShapeDtypeStruct((8, count * columns), jnp.int32),
                    *shapes,
                ],
                in_specs=[SMEM, SMEM, VMEM, VMEM, VMEM] + [VMEM] * count,
                out_specs=[VMEM] * (2 + len(steps)),
                scratch_shapes=[pltpu.VMEM((count, body, head_dim), jnp.bfloat16), scores],
                compiler_params=params,
                cost_estimate=cost,
            )(
                lengths, order, staged_keys, staged_values, spread,
                *[arrived[s] if s else packed for s in first_order(count)],
            )
            gathered = (asked, counts)
        else:
            parts = pl.pallas_call(
                functools.partial(next_kernel, start=start, scaling=scaling),
                out_shape=shapes,
                in_specs=[SMEM, VMEM, VMEM, VMEM, VMEM],
                out_specs=[VMEM] * len(steps),
                scratch_shapes=[scores],
                compiler_params=params,
                cost_estimate=cost,
            )(lengths, staged_keys, staged_values, *gathered)
        start += wide
        for step, part in zip(steps, parts):
            sent[step] = part if step == 0 else lax.ppermute(part, "blk", shift_pairs(count, step))

    state = []
    joins = join_plan(plan)
    for number, steps in enumerate(joins):
        last = number == len(joins) - 1
        shape = (
            jax.ShapeDtypeStruct((1, rows, heads, head_dim), jnp.bfloat16)
            if last
            else [
                jax.ShapeDtypeStruct((kv_heads, head_dim, columns), jnp.float32),
                jax.ShapeDtypeStruct((kv_heads, 8, columns), jnp.float32),
            ]
        )
        state = pl.pallas_call(
            functools.partial(
                settle_kernel, messages=len(steps), first=not state, last=last,
                kv_heads=kv_heads, width=head_dim, group=group,
            ),
            out_shape=shape,
            in_specs=[VMEM] * (len(steps) + len(state)),
            out_specs=VMEM if last else [VMEM, VMEM],
            compiler_params=pltpu.CompilerParams(vmem_limit_bytes=8 << 20),
            cost_estimate=cost_of(JOIN_COST),
        )(*[sent[step] for step in steps], *state)
    return state


def solution(mesh):
    placed = (
        P(("groups", "beam"), "blk", "heads", None),
        P(("groups", "beam"), "blk"),
        P(("groups", "beam"), None),
        P(("groups", "blk")),
        P(("groups", "blk"), "heads", None, None),
        P(("groups", "blk"), "heads", None, None),
    )
    return jax.shard_map(
        per_device,
        mesh=mesh,
        in_specs=placed,
        out_specs=P(("groups", "beam"), "blk", "heads", None),
        check_vma=False,
    )
```
